128 devices in a mesh: tok: 4 (over x_lo, core), wid: 8 (over z, x_hi), hid: 4 (over y).
Axes of the slice: x: 4 (x_hi: 2, x_lo: 2; x = x_hi * 2 + x_lo), y: 4, z: 4, core: 2. Of those that a mesh axis runs over, the one named last changes fastest.
Arguments:
- tokens: bfloat16 [1024, 6144], P(('tok', 'hid'), 'wid'), may hold values from -6 to 6
- up_weight: bfloat16 [6144, 24576], P('wid', ('hid', 'tok')), may hold values from -0.109375 to 0.109375
- down_weight: bfloat16 [24576, 6144], P(('hid', 'tok'), 'wid'), may hold values from -0.0546875 to 0.0546875
- cotangent: bfloat16 [1024, 6144], P(('tok', 'hid'), 'wid'), may hold values from -6 to 6
Outputs:
- layer_out: bfloat16 [1024, 6144], P(('tok', 'hid'), 'wid')
- tokens_grad: bfloat16 [1024, 6144], P(('tok', 'hid'), 'wid')
- up_grad: bfloat16 [6144, 24576], P('wid', ('hid', 'tok'))
- down_grad: bfloat16 [24576, 6144], P(('hid', 'tok'), 'wid')
The draws below stay inside these ranges and needn't reach their ends.
All inputs are finite; a program needn't handle non-finite values.
Results may differ from the reference program's by a relative error of at most 0.025.
Values may be sent and summed in bfloat16 or wider, within the bound.
No kernel may reach another device: no remote copies, remote signals or barrier semaphores. Data moves between devices by JAX's collectives and lax.ppermute only.
A program may use at most 128 MiB of HBM per device.

```python
import math
import jax
import jax.numpy as jnp
from jax import lax

D = 6144
FF = 24576
TOK_DEV = 256
TOKENS = 1024
N_TOK = 4
N_WID = 8


def spiked(result, key, source, target, blocks, factor):
    def block_of(dim):
        return (jnp.arange(result.shape[dim]) // (result.shape[dim] // blocks)).reshape((-1,) + (1,) * (result.ndim - 1 - dim))

    first = jax.random.permutation(key, blocks)[block_of(target)]
    other_side = (block_of(target) + blocks // 2) % blocks
    return jnp.where((block_of(source) == first) | (block_of(source) == other_side), factor * result, result)


def levels(own_key, extent, shards, smallest, top_value):
    gain = 1.0
    for position, parts in shards:
        draws = jax.random.uniform(jax.random.fold_in(jax.random.fold_in(own_key, 6), position), (parts,), jnp.float32, smallest / len(shards), top_value / len(shards))
        gain = gain * jnp.repeat(jnp.exp(draws), extent[position] // parts).reshape((-1,) + (1,) * (len(extent) - 1 - position))
    return gain


def gaussian(stream_key, dims, scale, reach, pieces=(), dtype=jnp.bfloat16):
    entries = scale * jax.random.normal(stream_key, dims, jnp.float32)
    if pieces:
        entries = entries * levels(stream_key, dims, pieces, -0.22, 0.18)
    return jnp.clip(entries, -reach, reach).astype(dtype)


def bell_draw_with(stream_key, shape, deviation, limit, split, heavy, dtype=jnp.bfloat16):
    array = deviation * jax.random.normal(stream_key, shape, jnp.float32)
    if split:
        array = array * levels(stream_key, shape, split, -0.22, 0.18)
    return jnp.clip(spiked(array, jax.random.fold_in(stream_key, 3), *heavy), -limit, limit).astype(dtype)


def setup_inputs(seed: int = 0) -> dict:
    arg_keys = jax.random.split(jax.random.key(seed), 5)
    tokens = gaussian(arg_keys[0], (TOKENS, D), 1.0, 6.0, ((0, 16), (1, 8)))
    up_weight = bell_draw_with(arg_keys[1], (D, FF), D ** -0.5, 0.109375, ((0, 8), (1, 16)), (0, 1, 16, 2.0))
    down_weight = bell_draw_with(arg_keys[2], (FF, D), FF ** -0.5, 0.0546875, ((0, 16), (1, 8)), (0, 1, 16, 2.0))
    cotangent = gaussian(arg_keys[3], (TOKENS, D), 1.0, 6.0, ((0, 16), (1, 8)))
    return {"tokens": tokens, "up_weight": up_weight, "down_weight": down_weight, "cotangent": cotangent}


tanh_scale = math.sqrt(2.0 / math.pi)
cubic_coef = 0.044715

def gelu_parts(preact):
    inner = tanh_scale * (preact + cubic_coef * preact * preact * preact)
    hyper = jnp.tanh(inner)
    activated = 0.5 * preact * (1.0 + hyper)
    derivative = 0.5 * (1.0 + hyper) + 0.5 * preact * (1.0 - hyper * hyper) * tanh_scale * (1.0 + 3.0 * cubic_coef * preact * preact)
    return (activated, derivative)

def rounded(value):
    low = lax.optimization_barrier(value.astype(jnp.bfloat16))
    return low.astype(jnp.float32)

def reference(tokens, up_weight, down_weight, cotangent):
    feat_block = D // N_WID
    preact = jnp.zeros((TOKENS, FF), jnp.float32)
    act_grad = jnp.zeros((TOKENS, FF), jnp.float32)
    for block in range(N_WID):
        lower = block * feat_block
        upper = lower + feat_block
        preact = preact + rounded(jnp.dot(tokens[:, lower:upper], up_weight[lower:upper, :], preferred_element_type=jnp.float32))
    activated_f, derivative = gelu_parts(preact)
    activated = activated_f.astype(jnp.bfloat16)
    layer_out = jnp.dot(activated, down_weight, preferred_element_type=jnp.float32).astype(jnp.bfloat16)
    for block in range(N_WID):
        lower = block * feat_block
        upper = lower + feat_block
        act_grad = act_grad + rounded(jnp.dot(cotangent[:, lower:upper], down_weight[:, lower:upper].T, preferred_element_type=jnp.float32))
    pre_grad = (act_grad * derivative).astype(jnp.bfloat16)
    tokens_grad = jnp.dot(pre_grad, up_weight.T, preferred_element_type=jnp.float32).astype(jnp.bfloat16)
    up_total = jnp.zeros((D, FF), jnp.float32)
    down_total = jnp.zeros((FF, D), jnp.float32)
    for block in range(N_TOK):
        lower = block * TOK_DEV
        upper = lower + TOK_DEV
        up_total = up_total + rounded(jnp.dot(tokens[lower:upper].T, pre_grad[lower:upper], preferred_element_type=jnp.float32))
        down_total = down_total + rounded(jnp.dot(activated[lower:upper].T, cotangent[lower:upper], preferred_element_type=jnp.float32))
    grad_scale = 1.0 / math.sqrt(TOKENS)
    up_grad = (up_total * grad_scale).astype(jnp.bfloat16)
    down_grad = (down_total * grad_scale).astype(jnp.bfloat16)
    return (layer_out, tokens_grad, up_grad, down_grad)
```

```python
import math

import jax
import jax.numpy as jnp
from jax import lax
from jax.sharding import PartitionSpec as P

tanh_scale = math.sqrt(2.0 / math.pi)
cubic_coef = 0.044715


def gelu_parts(preact):
    inner = tanh_scale * (preact + cubic_coef * preact * preact * preact)
    hyper = jnp.tanh(inner)
    activated = 0.5 * preact * (1.0 + hyper)
    derivative = 0.5 * (1.0 + hyper) + 0.5 * preact * (1.0 - hyper * hyper) * tanh_scale * (
        1.0 + 3.0 * cubic_coef * preact * preact
    )
    return (activated, derivative)


def contract(left, right, left_dim, right_dim):
    return lax.dot_general(
        left,
        right,
        (((left_dim,), (right_dim,)), ((), ())),
        preferred_element_type=jnp.float32,
    )


def local(tokens, up_weight, down_weight, cotangent):
    rows = ("tok", "hid")
    tok_all = lax.all_gather(tokens, rows, axis=0, tiled=True)
    cot_all = lax.all_gather(cotangent, rows, axis=0, tiled=True)
    pre_terms = contract(tok_all, up_weight, 1, 0).astype(jnp.bfloat16)
    preact = lax.psum_scatter(pre_terms, "wid", scatter_dimension=0, tiled=True)
    grad_terms = contract(cot_all, down_weight, 1, 1).astype(jnp.bfloat16)
    act_grad = lax.psum_scatter(grad_terms, "wid", scatter_dimension=0, tiled=True)
    activated, derivative = gelu_parts(preact.astype(jnp.float32))
    act_block = lax.all_gather(activated.astype(jnp.bfloat16), "wid", axis=0, tiled=True)
    pre_grad = (act_grad.astype(jnp.float32) * derivative).astype(jnp.bfloat16)
    hgrad_block = lax.all_gather(pre_grad, "wid", axis=0, tiled=True)
    out_terms = contract(act_block, down_weight, 1, 0).astype(jnp.bfloat16)
    layer_out = lax.psum_scatter(out_terms, rows, scatter_dimension=0, tiled=True)
    back_terms = contract(hgrad_block, up_weight, 1, 1).astype(jnp.bfloat16)
    tokens_grad = lax.psum_scatter(back_terms, rows, scatter_dimension=0, tiled=True)
    grad_scale = 1.0 / math.sqrt(tok_all.shape[0])
    down_grad = (contract(act_block, cot_all, 0, 0) * grad_scale).astype(jnp.bfloat16)
    up_grad = (contract(tok_all, hgrad_block, 0, 0) * grad_scale).astype(jnp.bfloat16)
    return (layer_out, tokens_grad, up_grad, down_grad)


def solution(mesh):
    in_specs = (
        P(("tok", "hid"), "wid"),
        P("wid", ("hid", "tok")),
        P(("hid", "tok"), "wid"),
        P(("tok", "hid"), "wid"),
    )
    out_specs = (
        P(("tok", "hid"), "wid"),
        P(("tok", "hid"), "wid"),
        P("wid", ("hid", "tok")),
        P(("hid", "tok"), "wid"),
    )
    return jax.shard_map(local, mesh=mesh, in_specs=in_specs, out_specs=out_specs, check_vma=False)
```

```python
import math

import jax
import jax.numpy as jnp
from jax import lax
from jax.sharding import Mesh
from jax.sharding import PartitionSpec as P

tanh_scale = math.sqrt(2.0 / math.pi)
cubic_coef = 0.044715
AXES = ("xl", "c", "z", "xh", "y")


def gelu_parts(preact):
    inner = tanh_scale * (preact + cubic_coef * preact * preact * preact)
    hyper = jnp.tanh(inner)
    activated = 0.5 * preact * (1.0 + hyper)
    derivative = 0.5 * (1.0 + hyper) + 0.5 * preact * (1.0 - hyper * hyper) * tanh_scale * (
        1.0 + 3.0 * cubic_coef * preact * preact
    )
    return (activated, derivative)


def contract(left, right, left_dim, right_dim):
    return lax.dot_general(
        left,
        right,
        (((left_dim,), (right_dim,)), ((), ())),
        preferred_element_type=jnp.float32,
    )


def low(value):
    return value.astype(jnp.bfloat16)


def wide(value):
    return value.astype(jnp.float32)


def send(value, axis, step):
    count = lax.axis_size(axis)
    return lax.ppermute(value, axis, [(i, (i + step) % count) for i in range(count)])


def relative(value):
    value = value.reshape(4, 2, 8, value.shape[-1])
    value = lax.dynamic_slice_in_dim(jnp.concatenate([value, value], 0), lax.axis_index("z"), 4, 0)
    return lax.dynamic_slice_in_dim(jnp.concatenate([value, value], 1), lax.axis_index("xh"), 2, 1)


def absolute(value):
    width = value.shape[-1]
    value = lax.dynamic_slice_in_dim(
        jnp.concatenate([value, value], 1), (2 - lax.axis_index("xh")) % 2, 2, 1
    )
    value = lax.dynamic_slice_in_dim(
        jnp.concatenate([value, value], 0), (4 - lax.axis_index("z")) % 4, 4, 0
    )
    return value.reshape(64, width)


def gather_groups(value):
    value = value[:, :, None]
    value = jnp.concatenate([value, send(value, "xl", 1)], 2)
    value = jnp.concatenate([value] + [send(value, "y", -d) for d in (1, 2, 3)], 2)
    return jnp.concatenate([value, send(value, "c", 1)], 2)


def scatter_groups(value):
    value = low(wide(value[:, :, :8]) + wide(send(value[:, :, 8:], "c", 1)))
    total = wide(value[:, :, :2])
    for d in (1, 2, 3):
        total = total + wide(send(value[:, :, 2 * d : 2 * d + 2], "y", d))
    value = low(total)
    return wide(value[:, :, 0]) + wide(send(value[:, :, 1], "xl", 1))


def scatter_wid(blocks):
    up_one = send(blocks[2][0], "z", 1)
    down_one = send(blocks[2][1], "z", -1)
    to_next = jnp.stack([low(wide(blocks[1][0]) + wide(up_one)), blocks[1][1]])
    to_last = jnp.stack([blocks[3][0], low(wide(blocks[3][1]) + wide(down_one))])
    total = wide(blocks[0]) + wide(send(to_next, "z", 1)) + wide(send(to_last, "z", -1))
    return total[0] + wide(send(low(total[1]), "xh", 1))


def gather_wid(value):
    own = jnp.stack([value, send(value, "xh", 1)])
    after = send(own, "z", -1)
    before = send(own, "z", 1)
    far = jnp.stack([send(after[0], "z", -1), send(before[1], "z", 1)])
    return [own, after, far, before]


def local(tokens, up_weight, down_weight, cotangent):
    width = tokens.shape[-1]
    hidden = up_weight.shape[-1]
    tok_all = gather_groups(relative(tokens)).reshape(4, 256, width)
    cot_all = gather_groups(relative(cotangent)).reshape(4, 256, width)
    order = (2, 1, 3, 0)
    pre_terms = [None] * 4
    grad_terms = [None] * 4
    for d in order:
        pre_terms[d] = low(contract(tok_all[d], up_weight, 1, 0)).reshape(2, 128, hidden)
    for d in order:
        grad_terms[d] = low(contract(cot_all[d], down_weight, 1, 1)).reshape(2, 128, hidden)
    preact = scatter_wid(pre_terms)
    act_grad = scatter_wid(grad_terms)
    activated, derivative = gelu_parts(preact)
    act = [part.reshape(256, hidden) for part in gather_wid(low(activated))]
    hgrad = [part.reshape(256, hidden) for part in gather_wid(low(act_grad * derivative))]
    out_terms = jnp.stack([low(contract(part, down_weight, 1, 0)) for part in act])
    layer_out = scatter_groups(out_terms.reshape(4, 2, 16, 8, width))
    back_terms = jnp.stack([low(contract(part, up_weight, 1, 1)) for part in hgrad])
    tokens_grad = scatter_groups(back_terms.reshape(4, 2, 16, 8, width))
    grad_scale = 1.0 / math.sqrt(1024.0)
    act_all = jnp.concatenate(act)
    hgrad_all = jnp.concatenate(hgrad)
    down_grad = low(contract(act_all, cot_all.reshape(1024, width), 0, 0) * grad_scale)
    up_grad = low(contract(tok_all.reshape(1024, width), hgrad_all, 0, 0) * grad_scale)
    return (absolute(low(layer_out)), absolute(low(tokens_grad)), up_grad, down_grad)


def solution(mesh):
    fine = Mesh(mesh.devices.reshape(2, 2, 4, 2, 4), AXES)
    rows = P(("xl", "c", "y"), ("z", "xh"))
    up_spec = P(("z", "xh"), ("y", "xl", "c"))
    down_spec = P(("y", "xl", "c"), ("z", "xh"))
    return jax.shard_map(
        local,
        mesh=fine,
        in_specs=(rows, up_spec, down_spec, rows),
        out_specs=(rows, rows, up_spec, down_spec),
        check_vma=False,
    )
```

```python
import functools
import math

import jax
import jax.numpy as jnp
from jax import lax
from jax.experimental import pallas as pl
from jax.experimental.pallas import tpu as pltpu
from jax.sharding import Mesh
from jax.sharding import PartitionSpec as P

tanh_scale = math.sqrt(2.0 / math.pi)
cubic_coef = 0.044715
AXES = ("xl", "c", "z", "xh", "y")


def gelu_parts(preact):
    inner = tanh_scale * (preact + cubic_coef * preact * preact * preact)
    hyper = jnp.tanh(inner)
    activated = 0.5 * preact * (1.0 + hyper)
    derivative = 0.5 * (1.0 + hyper) + 0.5 * preact * (1.0 - hyper * hyper) * tanh_scale * (
        1.0 + 3.0 * cubic_coef * preact * preact
    )
    return (activated, derivative)


def contract(left, right, left_dim, right_dim):
    return lax.dot_general(
        left,
        right,
        (((left_dim,), (right_dim,)), ((), ())),
        preferred_element_type=jnp.float32,
    )


def product_kernel(dim, *refs):
    count = (len(refs) - 1) // 2
    right = refs[count][...]
    for left_ref, out_ref in zip(refs[:count], refs[count + 1 :], strict=True):
        out_ref[...] = lax.dot_general(
            left_ref[...], right, (((1,), (dim,)), ((), ())), preferred_element_type=jnp.float32
        ).astype(out_ref.dtype)


def products(lefts, right, dim):
    rows, depth = lefts[0].shape
    total = right.shape[1 - dim]
    width = total // 3
    shape = (depth, width) if dim == 0 else (width, depth)
    return pl.pallas_call(
        functools.partial(product_kernel, dim),
        grid=(3,),
        out_shape=[jax.ShapeDtypeStruct((rows, total), jnp.bfloat16) for _ in lefts],
        in_specs=[pl.BlockSpec((rows, depth), lambda i: (0, 0)) for _ in lefts]
        + [pl.BlockSpec(shape, (lambda i: (0, i)) if dim == 0 else (lambda i: (i, 0)))],
        out_specs=[pl.BlockSpec((rows, width), lambda i: (0, i)) for _ in lefts],
        compiler_params=pltpu.CompilerParams(vmem_limit_bytes=32 * 2**20),
        cost_estimate=pl.CostEstimate(flops=1024, bytes_accessed=1024, transcendentals=0),
    )(*lefts, right)


def low(value):
    return value.astype(jnp.bfloat16)


def wide(value):
    return value.astype(jnp.float32)


def send(value, axis, step):
    count = lax.axis_size(axis)
    return lax.ppermute(value, axis, [(i, (i + step) % count) for i in range(count)])


def relative(value):
    value = value.reshape(4, 2, 8, value.shape[-1])
    value = lax.dynamic_slice_in_dim(jnp.concatenate([value, value], 0), lax.axis_index("z"), 4, 0)
    return lax.dynamic_slice_in_dim(jnp.concatenate([value, value], 1), lax.axis_index("xh"), 2, 1)


def absolute(value):
    width = value.shape[-1]
    value = lax.dynamic_slice_in_dim(
        jnp.concatenate([value, value], 1), (2 - lax.axis_index("xh")) % 2, 2, 1
    )
    value = lax.dynamic_slice_in_dim(
        jnp.concatenate([value, value], 0), (4 - lax.axis_index("z")) % 4, 4, 0
    )
    return value.reshape(64, width)


def after(kept, value, *others):
    value, others = lax.optimization_barrier((value, others))
    kept.extend(jax.tree.leaves(others))
    return value


def outer_kernel(count, scale, *refs):
    total = 0.0
    for left_ref, right_ref in zip(refs[:count], refs[count : 2 * count], strict=True):
        total = total + lax.dot_general(
            left_ref[...],
            right_ref[...],
            (((0,), (0,)), ((), ())),
            preferred_element_type=jnp.float32,
        )
    refs[-1][...] = (total * scale).astype(jnp.bfloat16)


def outer(lefts, rights, scale, kept=()):
    depth, rows = lefts[0].shape
    total = rights[0].shape[1]
    if rows > total:
        block = rows // 3
        left_spec = pl.BlockSpec((depth, block), lambda i: (0, i))
        right_spec = pl.BlockSpec((depth, total), lambda i: (0, 0))
        out_spec = pl.BlockSpec((block, total), lambda i: (i, 0))
    else:
        block = total // 3
        left_spec = pl.BlockSpec((depth, rows), lambda i: (0, 0))
        right_spec = pl.BlockSpec((depth, block), lambda i: (0, i))
        out_spec = pl.BlockSpec((rows, block), lambda i: (0, i))
    return pl.pallas_call(
        functools.partial(outer_kernel, len(lefts), scale),
        grid=(3,),
        out_shape=jax.ShapeDtypeStruct((rows, total), jnp.bfloat16),
        in_specs=[left_spec] * len(lefts)
        + [right_spec] * len(rights)
        + [pl.BlockSpec(memory_space=pl.ANY)] * len(kept),
        out_specs=out_spec,
        compiler_params=pltpu.CompilerParams(vmem_limit_bytes=48 * 2**20),
        cost_estimate=pl.CostEstimate(flops=1024, bytes_accessed=1024, transcendentals=0),
    )(*lefts, *rights, *kept)


def together(*values):
    return lax.optimization_barrier(values)


def gather_x(value):
    value = value[:, :, None]
    return jnp.concatenate([value, send(value, "xl", 1)], 2)


def gather_y(value):
    return [value] + [send(value, "y", -d) for d in (1, 2, 3)]


def send_blocks(value, axis, step):
    return jnp.concatenate([send(value[i : i + 1], axis, step) for i in range(value.shape[0])])


def gather_c(parts):
    value = jnp.concatenate(parts, 2)
    return [
        jnp.concatenate([block, send(block, "c", 1)], 1).reshape(256, block.shape[-1])
        for block in value
    ]


def scatter_c(value):
    return low(wide(value[:, :, :8]) + wide(send_blocks(value[:, :, 8:], "c", 1)))


def scatter_y(value):
    return [value[:, :, :2]] + [send(value[:, :, 2 * d : 2 * d + 2], "y", d) for d in (1, 2, 3)]


def scatter_x(parts):
    value = low(sum(wide(part) for part in parts))
    return value[:, :, 0], send(value[:, :, 1], "xl", 1)


def wid_first(block):
    return send(block[0], "z", 1), send(block[1], "z", -1)


def wid_second_terms(blocks, first):
    to_next = blocks[1].at[0].set(low(wide(blocks[1][0]) + wide(first[0])))
    to_last = blocks[3].at[1].set(low(wide(blocks[3][1]) + wide(first[1])))
    return to_next, to_last


def wid_second(pair):
    return send(pair[0], "z", 1), send(pair[1], "z", -1)


def wid_third(blocks, second):
    parts = [blocks[0], *second]
    other = low(sum(wide(part[1]) for part in parts))
    return sum(wide(part[0]) for part in parts), other


def local(tokens, up_weight, down_weight, cotangent):
    width = tokens.shape[-1]
    hidden = up_weight.shape[-1]
    grad_scale = 1.0 / math.sqrt(1024.0)

    def terms(lefts, right, dim):
        return [r.reshape(2, 128, hidden) for r in products(lefts, right, dim)]

    def out_terms(parts, right, dim):
        parts = [p.reshape(256, hidden) for p in parts]
        return jnp.stack(products(parts, right, dim)).reshape(-1, 2, 16, 8, width)

    kept = []
    wait = functools.partial(after, kept)
    tok_rel = relative(tokens)
    far_x = gather_x(tok_rel[2:3])
    far_y = gather_y(far_x)
    rest_x = gather_x(jnp.stack([tok_rel[0], tok_rel[1], tok_rel[3]]))
    cot_x = gather_x(relative(cotangent))
    rest_y = gather_y(wait(rest_x, far_y))
    tok_far = gather_c(far_y)
    pre_far = terms([tok_far[0]], up_weight, 0)[0]
    pre_first = wid_first(pre_far)
    tok_rest = gather_c(wait(rest_y, pre_far))
    pre_own, pre_next, pre_last = terms(list(tok_rest), up_weight, 0)
    pre = [pre_own, pre_next, pre_far, pre_last]
    cot_y = gather_y(wait(cot_x, pre_own))
    pre_pair = wid_second_terms(pre, pre_first)
    pre_second = wid_second(pre_pair)
    cot_all = gather_c(wait(cot_y, pre_pair))
    grad = terms(list(cot_all), down_weight, 1)
    grad_first = wid_first(grad[2])
    pre_here, pre_other = wid_third(pre, pre_second)
    grad_first = wait(grad_first, pre_other)
    grad_pair = wid_second_terms(grad, grad_first)
    grad_second = wid_second(grad_pair)
    pre_there = send(pre_other, "xh", 1)
    activated, derivative = gelu_parts(pre_here + wide(pre_there))
    act_here = low(activated)
    act_there = send(act_here, "xh", 1)
    act_here_near = together(send(act_here, "z", -1), send(act_here, "z", 1))
    grad_second = wait(grad_second, act_there)
    act_there_near = together(send(act_there, "z", -1), send(act_there, "z", 1))
    grad_here, grad_other = wid_third(grad, grad_second)
    grad_there = send(grad_other, "xh", 1)
    act_far_here = send(act_here_near[0], "z", -1)
    hgrad_here = low((grad_here + wide(grad_there)) * derivative)
    hgrad_there = send(hgrad_here, "xh", 1)
    hgrad_here_near = together(send(hgrad_here, "z", -1), send(hgrad_here, "z", 1))
    act_there_near = wait(act_there_near, hgrad_here)
    act_far_there = send(act_there_near[1], "z", 1)
    act_far_there = wait(act_far_there, hgrad_there)
    act = [
        jnp.stack(pair)
        for pair in (
            (act_here, act_there),
            (act_here_near[0], act_there_near[0]),
            (act_far_here, act_far_there),
            (act_here_near[1], act_there_near[1]),
        )
    ]
    hgrad_there_near = together(send(hgrad_there, "z", -1), send(hgrad_there, "z", 1))
    out_c = scatter_c(out_terms(act, down_weight, 0))
    out_y = scatter_y(out_c)
    hgrad_far_here = send(hgrad_here_near[0], "z", -1)
    hgrad_far_there = send(hgrad_there_near[1], "z", 1)
    act_parts = wait([part.reshape(256, hidden) for part in act], out_c)
    down_grad = outer(act_parts, list(cot_all), grad_scale)
    out_y = wait(out_y, hgrad_far_here, hgrad_there_near, down_grad)
    hgrad = [
        jnp.stack(pair)
        for pair in (
            (hgrad_here, hgrad_there),
            (hgrad_here_near[0], hgrad_there_near[0]),
            (hgrad_far_here, hgrad_far_there),
            (hgrad_here_near[1], hgrad_there_near[1]),
        )
    ]
    near_c = scatter_c(out_terms([hgrad[0], hgrad[1], hgrad[3]], up_weight, 1))
    out_parts = scatter_x(out_y)
    near_y = scatter_y(near_c)
    hgrad_far = wait(hgrad[2], near_y)
    far_c = scatter_c(out_terms([hgrad_far], up_weight, 1))
    far_y = scatter_y(far_c)
    hgrad_parts = wait([part.reshape(256, hidden) for part in hgrad], far_c)
    tok_parts = [tok_rest[0], tok_rest[1], tok_far[0], tok_rest[2]]
    up_grad = outer(tok_parts, hgrad_parts, grad_scale, kept)
    back_parts = scatter_x(
        [jnp.concatenate([n[:2], f, n[2:]]) for n, f in zip(near_y, far_y, strict=True)]
    )
    layer_out = low(wide(out_parts[0]) + wide(out_parts[1]))
    tokens_grad = low(wide(back_parts[0]) + wide(back_parts[1]))
    return (absolute(layer_out), absolute(tokens_grad), up_grad, down_grad)


def solution(mesh):
    fine = Mesh(mesh.devices.reshape(2, 2, 4, 2, 4), AXES)
    rows = P(("xl", "c", "y"), ("z", "xh"))
    up_spec = P(("z", "xh"), ("y", "xl", "c"))
    down_spec = P(("y", "xl", "c"), ("z", "xh"))
    return jax.shard_map(
        local,
        mesh=fine,
        in_specs=(rows, up_spec, down_spec, rows),
        out_specs=(rows, rows, up_spec, down_spec),
        check_vma=False,
    )
```

```python
import functools
import math

import jax
import jax.numpy as jnp
from jax import lax
from jax.experimental import pallas as pl
from jax.experimental.pallas import tpu as pltpu
from jax.sharding import Mesh
from jax.sharding import PartitionSpec as P

tanh_scale = math.sqrt(2.0 / math.pi)
cubic_coef = 0.044715
AXES = ("xl", "c", "z", "xh", "y")


def gelu_parts(preact):
    inner = tanh_scale * (preact + cubic_coef * preact * preact * preact)
    hyper = jnp.tanh(inner)
    activated = 0.5 * preact * (1.0 + hyper)
    derivative = 0.5 * (1.0 + hyper) + 0.5 * preact * (1.0 - hyper * hyper) * tanh_scale * (
        1.0 + 3.0 * cubic_coef * preact * preact
    )
    return (activated, derivative)


def contract(left, right, left_dim, right_dim):
    return lax.dot_general(
        left,
        right,
        (((left_dim,), (right_dim,)), ((), ())),
        preferred_element_type=jnp.float32,
    )


def product_kernel(dim, *refs):
    count = (len(refs) - 1) // 2
    right = refs[count][...]
    for left_ref, out_ref in zip(refs[:count], refs[count + 1 :], strict=True):
        out_ref[...] = lax.dot_general(
            left_ref[...], right, (((1,), (dim,)), ((), ())), preferred_element_type=jnp.float32
        ).astype(out_ref.dtype)


def products(lefts, right, dim):
    rows, depth = lefts[0].shape
    total = right.shape[1 - dim]
    width = total // 3
    shape = (depth, width) if dim == 0 else (width, depth)
    return pl.pallas_call(
        functools.partial(product_kernel, dim),
        grid=(3,),
        out_shape=[jax.ShapeDtypeStruct((rows, total), jnp.bfloat16) for _ in lefts],
        in_specs=[pl.BlockSpec((rows, depth), lambda i: (0, 0)) for _ in lefts]
        + [pl.BlockSpec(shape, (lambda i: (0, i)) if dim == 0 else (lambda i: (i, 0)))],
        out_specs=[pl.BlockSpec((rows, width), lambda i: (0, i)) for _ in lefts],
        compiler_params=pltpu.CompilerParams(vmem_limit_bytes=32 * 2**20),
        cost_estimate=pl.CostEstimate(flops=1024, bytes_accessed=1024, transcendentals=0),
    )(*lefts, right)


def low(value):
    return value.astype(jnp.bfloat16)


def wide(value):
    return value.astype(jnp.float32)


def send(value, axis, step):
    count = lax.axis_size(axis)
    return lax.ppermute(value, axis, [(i, (i + step) % count) for i in range(count)])


def relative(value):
    value = value.reshape(4, 2, 8, value.shape[-1])
    value = lax.dynamic_slice_in_dim(jnp.concatenate([value, value], 0), lax.axis_index("z"), 4, 0)
    return lax.dynamic_slice_in_dim(jnp.concatenate([value, value], 1), lax.axis_index("xh"), 2, 1)


def absolute(value):
    width = value.shape[-1]
    value = lax.dynamic_slice_in_dim(
        jnp.concatenate([value, value], 1), (2 - lax.axis_index("xh")) % 2, 2, 1
    )
    value = lax.dynamic_slice_in_dim(
        jnp.concatenate([value, value], 0), (4 - lax.axis_index("z")) % 4, 4, 0
    )
    return value.reshape(64, width)


def after(kept, value, *others):
    value, others = lax.optimization_barrier((value, others))
    kept.extend(jax.tree.leaves(others))
    return value


def outer_kernel(count, scale, *refs):
    total = 0.0
    for left_ref, right_ref in zip(refs[:count], refs[count : 2 * count], strict=True):
        total = total + lax.dot_general(
            left_ref[...],
            right_ref[...],
            (((0,), (0,)), ((), ())),
            preferred_element_type=jnp.float32,
        )
    refs[-1][...] = (total * scale).astype(jnp.bfloat16)


def outer(lefts, rights, scale, kept=()):
    depth, rows = lefts[0].shape
    total = rights[0].shape[1]
    if rows > total:
        block = rows // 3
        left_spec = pl.BlockSpec((depth, block), lambda i: (0, i))
        right_spec = pl.BlockSpec((depth, total), lambda i: (0, 0))
        out_spec = pl.BlockSpec((block, total), lambda i: (i, 0))
    else:
        block = total // 3
        left_spec = pl.BlockSpec((depth, rows), lambda i: (0, 0))
        right_spec = pl.BlockSpec((depth, block), lambda i: (0, i))
        out_spec = pl.BlockSpec((rows, block), lambda i: (0, i))
    return pl.pallas_call(
        functools.partial(outer_kernel, len(lefts), scale),
        grid=(3,),
        out_shape=jax.ShapeDtypeStruct((rows, total), jnp.bfloat16),
        in_specs=[left_spec] * len(lefts)
        + [right_spec] * len(rights)
        + [pl.BlockSpec(memory_space=pl.ANY)] * len(kept),
        out_specs=out_spec,
        compiler_params=pltpu.CompilerParams(vmem_limit_bytes=48 * 2**20),
        cost_estimate=pl.CostEstimate(flops=2_400_000_000, bytes_accessed=1024, transcendentals=0),
    )(*lefts, *rights, *kept)


def together(*values):
    return lax.optimization_barrier(values)


def gather_x(value):
    value = value[:, :, None]
    return jnp.concatenate([value, send(value, "xl", 1)], 2)


def gather_y(value):
    return [value] + [send(value, "y", -d) for d in (1, 2, 3)]


def send_blocks(value, axis, step):
    return jnp.concatenate([send(value[i : i + 1], axis, step) for i in range(value.shape[0])])


def gather_c(parts, whole=False):
    value = jnp.concatenate(parts, 2)
    if whole:
        value = jnp.concatenate([value, send(value, "c", 1)], 2)
        return [block.reshape(256, block.shape[-1]) for block in value]
    return [
        jnp.concatenate([block, send(block, "c", 1)], 1).reshape(256, block.shape[-1])
        for block in value
    ]


def scatter_c(value, whole=False):
    return low(wide(value[:, :, :8]) + wide((send if whole else send_blocks)(value[:, :, 8:], "c", 1)))


def scatter_y(value):
    return [value[:, :, :2]] + [send(value[:, :, 2 * d : 2 * d + 2], "y", d) for d in (1, 2, 3)]


def scatter_x(parts):
    value = low(sum(wide(part) for part in parts))
    return value[:, :, 0], send(value[:, :, 1], "xl", 1)


def wid_first(block):
    return send(block[0], "z", 1), send(block[1], "z", -1)


def wid_second_terms(blocks, first):
    to_next = blocks[1].at[0].set(low(wide(blocks[1][0]) + wide(first[0])))
    to_last = blocks[3].at[1].set(low(wide(blocks[3][1]) + wide(first[1])))
    return to_next, to_last


def wid_second(pair):
    return send(pair[0], "z", 1), send(pair[1], "z", -1)


def wid_third(blocks, second):
    parts = [blocks[0], *second]
    other = low(sum(wide(part[1]) for part in parts))
    return sum(wide(part[0]) for part in parts), other


def local(tokens, up_weight, down_weight, cotangent):
    width = tokens.shape[-1]
    hidden = up_weight.shape[-1]
    grad_scale = 1.0 / math.sqrt(1024.0)

    def terms(lefts, right, dim):
        return [r.reshape(2, 128, hidden) for r in products(lefts, right, dim)]

    def out_terms(parts, right, dim):
        parts = [p.reshape(256, hidden) for p in parts]
        return jnp.stack(products(parts, right, dim)).reshape(-1, 2, 16, 8, width)

    kept = []
    wait = functools.partial(after, kept)
    tok_rel = relative(tokens)
    far_x = gather_x(tok_rel[2:3])
    far_y = gather_y(far_x)
    rest_x = gather_x(jnp.concatenate([tok_rel[1:2], tok_rel[3:], tok_rel[:1]]))
    cot_x = gather_x(relative(cotangent))
    rest_y = gather_y(wait(rest_x, far_y))
    tok_far = gather_c(far_y, True)
    pre_far = terms([tok_far[0]], up_weight, 0)[0]
    pre_first = wid_first(pre_far)
    rest_y = wait(rest_y, pre_far)
    rest = gather_c(rest_y, True)
    tok_rest = [rest[2], rest[0], rest[1]]
    pre_own, pre_next, pre_last = terms(tok_rest, up_weight, 0)
    pre = [pre_own, pre_next, pre_far, pre_last]
    cot_y = gather_y(wait(cot_x, pre_far))
    pre_pair = wid_second_terms(pre, pre_first)
    pre_second = wid_second(pre_pair)
    cot_all = gather_c(cot_y, True)
    grad = terms(cot_all, down_weight, 1)
    grad_first = wid_first(grad[2])
    pre_here, pre_other = wid_third(pre, pre_second)
    pre_there = send(pre_other, "xh", 1)
    grad_first = wait(grad_first, pre_other)
    grad_pair = wid_second_terms(grad, grad_first)
    grad_second = wid_second(grad_pair)
    activated, derivative = gelu_parts(pre_here + wide(pre_there))
    act_here = low(activated)
    act_there = send(act_here, "xh", 1)
    act_here_near = together(send(act_here, "z", -1), send(act_here, "z", 1))
    grad_second = wait(grad_second, act_there)
    act_there_near = together(send(act_there, "z", -1), send(act_there, "z", 1))
    grad_here, grad_other = wid_third(grad, grad_second)
    grad_there = send(grad_other, "xh", 1)
    act_far_here = send(act_here_near[0], "z", -1)
    hgrad_here = low((grad_here + wide(grad_there)) * derivative)
    hgrad_there = send(hgrad_here, "xh", 1)
    hgrad_here_near = together(send(hgrad_here, "z", -1), send(hgrad_here, "z", 1))
    act_there_near = wait(act_there_near, hgrad_here)
    act_far_there = send(act_there_near[1], "z", 1)
    hgrad_far_here = send(hgrad_here_near[0], "z", -1)
    hgrad_there_near = together(send(hgrad_there, "z", -1), send(hgrad_there, "z", 1))
    hgrad_far_there = send(hgrad_there_near[1], "z", 1)
    act = [
        jnp.stack(pair)
        for pair in (
            (act_here, act_there),
            (act_here_near[0], act_there_near[0]),
            (act_far_here, act_far_there),
            (act_here_near[1], act_there_near[1]),
        )
    ]
    out_c = scatter_c(out_terms(act, down_weight, 0))
    out_y = scatter_y(out_c)
    act_parts = wait([part.reshape(256, hidden) for part in act], out_c)
    down_grad = outer(act_parts, cot_all, grad_scale)
    out_y = wait(out_y, hgrad_far_here, hgrad_there_near, down_grad)
    hgrad = [
        jnp.stack(pair)
        for pair in (
            (hgrad_here, hgrad_there),
            (hgrad_here_near[0], hgrad_there_near[0]),
            (hgrad_far_here, hgrad_far_there),
            (hgrad_here_near[1], hgrad_there_near[1]),
        )
    ]
    near_c = scatter_c(out_terms([hgrad[0], hgrad[1], hgrad[3]], up_weight, 1))
    out_parts = scatter_x(out_y)
    near_y = scatter_y(near_c)
    hgrad_last = wait(hgrad[2], near_y)
    far_c = scatter_c(out_terms([hgrad_last], up_weight, 1))
    far_y = scatter_y(far_c)
    hgrad_parts = wait([part.reshape(256, hidden) for part in hgrad], far_c)
    tok_parts = [tok_rest[0], tok_rest[1], tok_far[0], tok_rest[2]]
    up_grad = outer(tok_parts, hgrad_parts, grad_scale, kept)
    back_parts = scatter_x(
        [jnp.concatenate([n[:2], f, n[2:]]) for n, f in zip(near_y, far_y, strict=True)]
    )
    layer_out = low(wide(out_parts[0]) + wide(out_parts[1]))
    tokens_grad = low(wide(back_parts[0]) + wide(back_parts[1]))
    return (absolute(layer_out), absolute(tokens_grad), up_grad, down_grad)

def solution(mesh):
    fine = Mesh(mesh.devices.reshape(2, 2, 4, 2, 4), AXES)
    rows = P(("xl", "c", "y"), ("z", "xh"))
    up_spec = P(("z", "xh"), ("y", "xl", "c"))
    down_spec = P(("y", "xl", "c"), ("z", "xh"))
    return jax.shard_map(
        local,
        mesh=fine,
        in_specs=(rows, up_spec, down_spec, rows),
        out_specs=(rows, rows, up_spec, down_spec),
        check_vma=False,
    )
```
